128 devices in a mesh: seq: 64 (over x, y, z_lo, core), fsdp: 2 (over z_hi).
Axes of the slice: x: 4, y: 4, z: 4 (z_hi: 2, z_lo: 2; z = z_hi * 2 + z_lo), core: 2. Of those that a mesh axis runs over, the one named last changes fastest.
Arguments:
- queries: bfloat16 [2, 8192, 8192], P('fsdp', 'seq'), may hold values from -10 to 10
- keys: bfloat16 [2, 8192, 1024], P('fsdp', 'seq'), may hold values from -10 to 10
- values: bfloat16 [2, 8192, 1024], P('fsdp', 'seq'), may hold values from -6 to 6
- out_grad: bfloat16 [2, 8192, 8192], P('fsdp', 'seq'), may hold values from -6 to 6
- doc_lengths: int32 [2, 64], P('fsdp'), may hold values from 1 to 1024, 8192 in all within a row
- inputs: bfloat16 [2, 8192, 4096], P('fsdp', 'seq'), may hold values from -16 to 16
- value_weight: bfloat16 [4096, 1024], P('fsdp'), may hold values from -0.1875 to 0.1875
Outputs:
- grad_queries: bfloat16 [2, 8192, 8192], P('fsdp', 'seq')
- grad_keys: bfloat16 [2, 8192, 1024], P('fsdp', 'seq')
- grad_values: bfloat16 [2, 8192, 1024], P('fsdp', 'seq')
- grad_inputs: bfloat16 [2, 8192, 4096], P('fsdp', 'seq')
- grad_weight: float32 [4096, 1024], P(('seq', 'fsdp'))
The draws below stay inside these ranges and needn't reach their ends.
Inputs may be any that keep to these rules, and one draw needn't show every extreme that they name: `doc_lengths`: each row lists the lengths of the 64 documents packed into one sequence, in order; they sum to 8192 and the longest is exactly 1024.
All inputs are finite; a program needn't handle non-finite values.
Results may differ from the reference program's by a relative error of at most 0.0079.
Values may be sent and summed in bfloat16 or wider, within the bound.
A program may use at most 192 MiB of HBM per device.

```python
import math
import jax
import jax.numpy as jnp
import numpy as np
from jax import lax

HEADS = 64
KV_HEADS = 8
HEAD_DIM = 128
DW = 4096
MAXDOC = 1024
SEQLEN = 8192
DOCS = 64
N_FSDP = 2


def drawn_pair(key):
    base = jax.random.fold_in(key, 7331)
    split_keys = jax.random.split(base, 2)
    shape_kv = (N_FSDP, SEQLEN, KV_HEADS, HEAD_DIM)
    query_draw = jnp.clip(jax.random.normal(split_keys[0], (N_FSDP, SEQLEN, HEADS, HEAD_DIM), jnp.float32), -6.0, 6.0)
    key_draw = jnp.clip(jax.random.normal(split_keys[1], shape_kv, jnp.float32), -6.0, 6.0)
    return (query_draw.reshape(N_FSDP, SEQLEN, HEADS * HEAD_DIM), key_draw.reshape(N_FSDP, SEQLEN, KV_HEADS * HEAD_DIM))


def draw_queries(key, part):
    return drawn_pair(key)[0].astype(jnp.bfloat16)


def draw_keys(key, part):
    return drawn_pair(key)[1].astype(jnp.bfloat16)


def spiked(array, own_key, source, target, parts, factor):
    def block_of(dim):
        return (jnp.arange(array.shape[dim]) // (array.shape[dim] // parts)).reshape((-1,) + (1,) * (array.ndim - 1 - dim))

    one_side = jax.random.permutation(own_key, parts)[block_of(target)]
    second = (block_of(target) + parts // 2) % parts
    return jnp.where((block_of(source) == one_side) | (block_of(source) == second), factor * array, array)


def steps_of(rng, dims, cuts, low, top_value):
    factor_of = 1.0
    for dim, blocks in cuts:
        heights = jax.random.uniform(jax.random.fold_in(jax.random.fold_in(rng, 6), dim), (blocks,), jnp.float32, low / len(cuts), top_value / len(cuts))
        factor_of = factor_of * jnp.repeat(jnp.exp(heights), dims[dim] // blocks).reshape((-1,) + (1,) * (len(dims) - 1 - dim))
    return factor_of


def length_profile(count, total, reach, slope):
    weights = [(1 << 20) // math.isqrt(grade ** slope) + 1 for grade in range(2, count + 1)]
    rest, given = total - reach - (count - 1), [1] * (count - 1)
    while rest > 0:
        candidates = [i for i in range(count - 1) if given[i] < reach]
        pool, remaining = sum([weights[i] for i in candidates]), rest
        for i in candidates:
            more = min(reach - given[i], max(1, remaining * weights[i] // pool), rest)
            given[i] = given[i] + more
            rest = rest - more
    return np.array([reach] + given)


def uneven_parts(key, count, total, reach, slope):
    if count == 2:
        one = jax.random.randint(key, (), max(1, total - reach), min(reach, total - 1) + 1)
        return jnp.stack([one, total - one])
    sizes = jnp.asarray(length_profile(count, total, reach, slope), jnp.int32)
    couples = (count - 1) // 2
    donor, taker = sizes[1:1 + 2 * couples:2], sizes[2:2 + 2 * couples:2]
    slack = jnp.minimum(donor - 1, reach - taker)
    shifted = jax.random.randint(jax.random.fold_in(key, 1), (couples,), 0, 1 << 20) % (slack + 1)
    sizes = sizes.at[1:1 + 2 * couples:2].set(donor - shifted).at[2:2 + 2 * couples:2].set(taker + shifted)
    return sizes[jax.random.permutation(jax.random.fold_in(key, 2), count)]


def centred(key, shape, deviation, most, pieces=(), held_as=jnp.bfloat16):
    loudness = steps_of(key, shape, pieces, -0.22, 0.18) if pieces else 1.0
    array = jax.random.normal(key, shape, jnp.float32) * deviation * loudness
    return jnp.minimum(jnp.maximum(array, -most), most).astype(held_as)


def heavy_noise(own_key, dims, scale, most, cuts, heavy, held_as=jnp.bfloat16):
    values = scale * jax.random.normal(own_key, dims, jnp.float32)
    if cuts:
        values = values * steps_of(own_key, dims, cuts, -0.22, 0.18)
    return jnp.clip(spiked(values, jax.random.fold_in(own_key, 3), *heavy), -most, most).astype(held_as)


def setup_inputs(seed: int = 0) -> dict:
    key_of = jax.random.split(jax.random.key(seed), 8)
    return {
        "queries": draw_queries(jax.random.fold_in(key_of[7], 71), 0),
        "keys": draw_keys(jax.random.fold_in(key_of[7], 71), 0),
        "values": centred(key_of[2], (N_FSDP, SEQLEN, KV_HEADS * HEAD_DIM), 1.0, 6.0, ((0, 2), (1, 64))),
        "out_grad": centred(key_of[3], (N_FSDP, SEQLEN, HEADS * HEAD_DIM), 1.0, 6.0, ((0, 2), (1, 64))),
        "doc_lengths": jax.vmap(lambda own: uneven_parts(own, DOCS, SEQLEN, MAXDOC, 2))(jax.random.split(key_of[4], N_FSDP)).reshape((N_FSDP, DOCS)).astype(jnp.int32),
        "inputs": heavy_noise(key_of[5], (N_FSDP, SEQLEN, DW), 1.0, 16.0, ((0, 2), (1, 64)), (1, 2, 64, 4.0)),
        "value_weight": centred(key_of[6], (DW, KV_HEADS * HEAD_DIM), (KV_HEADS * HEAD_DIM) ** -0.5, 0.1875, ((0, 2),)),
    }


masked_value = -1e+30

def document_ids(lengths, seqlen_value):
    bounds = jnp.cumsum(lengths).astype(jnp.int32)
    positions = jnp.arange(seqlen_value, dtype=jnp.int32)
    return lax.optimization_barrier(jnp.sum((positions[:, None] >= bounds[None, :]).astype(jnp.int32), axis=1)).astype(jnp.int32)

def head_backward(query_one, key_one, value_one, grad_one, doc_ids, block_rows, reach_back):
    seq_rows, head_width = query_one.shape
    score_scale = 1.0 / math.sqrt(head_width)
    slab_rows = block_rows + reach_back
    pad_keys = jnp.concatenate([jnp.zeros((reach_back, head_width), key_one.dtype), key_one], axis=0)
    pad_values = jnp.concatenate([jnp.zeros((reach_back, head_width), value_one.dtype), value_one], axis=0)
    pad_docs = jnp.concatenate([jnp.full((reach_back,), -1, jnp.int32), doc_ids], axis=0)
    query_offsets = jnp.arange(block_rows, dtype=jnp.int32)
    key_offsets = jnp.arange(slab_rows, dtype=jnp.int32)

    def visit(state_pair, offset):
        key_grad, value_grad = state_pair
        query_block = lax.dynamic_slice_in_dim(query_one, offset, block_rows, 0)
        grad_block = lax.dynamic_slice_in_dim(grad_one, offset, block_rows, 0)
        key_block = lax.dynamic_slice_in_dim(pad_keys, offset, slab_rows, 0)
        value_block = lax.dynamic_slice_in_dim(pad_values, offset, slab_rows, 0)
        query_docs = lax.dynamic_slice_in_dim(doc_ids, offset, block_rows, 0)
        key_docs = lax.dynamic_slice_in_dim(pad_docs, offset, slab_rows, 0)
        allowed = (query_docs[:, None] == key_docs[None, :]) & (key_offsets[None, :] <= query_offsets[:, None] + reach_back)
        scores = lax.dot_general(query_block, key_block, (((1,), (1,)), ((), ())), preferred_element_type=jnp.float32) * score_scale
        scores = jnp.where(allowed, scores, masked_value)
        row_max = lax.optimization_barrier(jnp.max(scores, axis=1, keepdims=True))
        weights = jnp.where(allowed, jnp.exp(scores - row_max), 0.0)
        probs = weights / lax.optimization_barrier(jnp.sum(weights, axis=1, keepdims=True))
        dprob = lax.dot_general(grad_block, value_block, (((1,), (1,)), ((), ())), preferred_element_type=jnp.float32)
        row_delta = lax.optimization_barrier(jnp.sum(probs * dprob, axis=1, keepdims=True))
        dscore = (probs * (dprob - row_delta)).astype(jnp.bfloat16)
        probs_low = probs.astype(jnp.bfloat16)
        query_grad = (jnp.dot(dscore, key_block, preferred_element_type=jnp.float32) * score_scale).astype(jnp.bfloat16)
        key_part = lax.dot_general(dscore, query_block, (((0,), (0,)), ((), ())), preferred_element_type=jnp.float32) * score_scale
        value_part = lax.dot_general(probs_low, grad_block, (((0,), (0,)), ((), ())), preferred_element_type=jnp.float32)
        key_grad = lax.dynamic_update_slice_in_dim(key_grad, lax.dynamic_slice_in_dim(key_grad, offset, slab_rows, 0) + key_part, offset, 0)
        value_grad = lax.dynamic_update_slice_in_dim(value_grad, lax.dynamic_slice_in_dim(value_grad, offset, slab_rows, 0) + value_part, offset, 0)
        return ((key_grad, value_grad), query_grad)
    empty_grads = jnp.zeros((seq_rows + reach_back, head_width), jnp.float32)
    offsets = jnp.arange(seq_rows // block_rows, dtype=jnp.int32) * block_rows
    (key_grad, value_grad), query_grads = lax.scan(visit, (empty_grads, empty_grads), offsets)
    return (query_grads.reshape(seq_rows, head_width), key_grad[reach_back:], value_grad[reach_back:])

def reference(queries, keys, values, out_grad, doc_lengths, inputs, value_weight):
    block_rows = min(512, SEQLEN)
    group_size = HEADS // KV_HEADS
    query_list, key_list, value_list, input_list = ([], [], [], [])
    weight_sum = jnp.zeros((DW, KV_HEADS * HEAD_DIM), jnp.float32)
    for sequence in range(N_FSDP):
        doc_ids = document_ids(doc_lengths[sequence], SEQLEN)
        query_seq = queries[sequence].reshape(SEQLEN, HEADS, HEAD_DIM)
        grad_seq = out_grad[sequence].reshape(SEQLEN, HEADS, HEAD_DIM)
        key_seq = keys[sequence].reshape(SEQLEN, KV_HEADS, HEAD_DIM)
        value_seq = values[sequence].reshape(SEQLEN, KV_HEADS, HEAD_DIM)

        def one_head(head_index):
            kv_index = head_index // group_size
            return head_backward(lax.dynamic_index_in_dim(query_seq, head_index, 1, keepdims=False), lax.dynamic_index_in_dim(key_seq, kv_index, 1, keepdims=False), lax.dynamic_index_in_dim(value_seq, kv_index, 1, keepdims=False), lax.dynamic_index_in_dim(grad_seq, head_index, 1, keepdims=False), doc_ids, block_rows, MAXDOC)
        query_grads, key_terms, value_terms = lax.map(one_head, jnp.arange(HEADS, dtype=jnp.int32))
        query_list.append(jnp.transpose(query_grads, (1, 0, 2)).reshape(SEQLEN, HEADS * HEAD_DIM))
        key_sum = key_terms.reshape(KV_HEADS, group_size, SEQLEN, HEAD_DIM).sum(axis=1).astype(jnp.bfloat16)
        value_sum = value_terms.reshape(KV_HEADS, group_size, SEQLEN, HEAD_DIM).sum(axis=1).astype(jnp.bfloat16)
        key_flat = jnp.transpose(key_sum, (1, 0, 2)).reshape(SEQLEN, KV_HEADS * HEAD_DIM)
        value_flat = jnp.transpose(value_sum, (1, 0, 2)).reshape(SEQLEN, KV_HEADS * HEAD_DIM)
        key_list.append(key_flat)
        value_list.append(value_flat)
        input_list.append(lax.dot_general(value_flat, value_weight, (((1,), (1,)), ((), ())), preferred_element_type=jnp.float32).astype(jnp.bfloat16))
        weight_sum = weight_sum + lax.dot_general(inputs[sequence], value_flat, (((0,), (0,)), ((), ())), preferred_element_type=jnp.float32)
    grad_weight = weight_sum * (1.0 / math.sqrt(N_FSDP * SEQLEN))
    return (jnp.stack(query_list), jnp.stack(key_list), jnp.stack(value_list), jnp.stack(input_list), grad_weight)
```

```python
import math

import jax
import jax.numpy as jnp
from jax import lax
from jax.experimental import pallas as pl
from jax.experimental.pallas import tpu as pltpu
from jax.sharding import PartitionSpec as P

D = 128
T = 256
W = 1280
HALF = 4
HB = 4
SCALE = 1.0 / math.sqrt(D)
EXP2 = math.log2(math.e) * SCALE
NT = (((1,), (1,)), ((), ()))
f32, bf16 = jnp.float32, jnp.bfloat16
MESH = pl.DeviceIdType.MESH
ANY = pl.BlockSpec(memory_space=pl.ANY)
VMEM = pl.BlockSpec(memory_space=pltpu.VMEM)


def position():
    p, f = lax.axis_index("seq"), lax.axis_index("fsdp")
    return p, f, p // 16, p // 4 % 4, p // 2 % 2, p % 2


def wrapped(p, by):
    return lax.rem(p + by + 64, 64)


def along_x(p, dx):
    return lax.rem(p + 16 * dx, 64)


def along_y(p, y, dy):
    return p - 4 * y + 4 * lax.rem(y + dy, 4)


def greet(devices):
    barrier = pltpu.get_barrier_semaphore()
    for device in devices:
        pl.semaphore_signal(barrier, inc=1, device_id=device, device_id_type=MESH)
    pl.semaphore_wait(barrier, len(devices))


def rows_of(index, size=T):
    return pl.ds(pl.multiple_of(index * size, size), size)


def gather_kernel(
    q_ref, do_ref, k_ref, v_ref, in_ref, w_ref, qx_ref, dox_ref, slab_ref, inx_ref, wx_ref, send, recv, near
):
    p, f, x, y, zl, k = position()
    sib = (p + 1 - 2 * k, f)
    zdev = (p + 2 - 4 * zl, f)
    up, down = (wrapped(p, 4), f), (wrapped(p, -4), f)
    fdev = (p, 1 - f)
    xs = [(along_x(p, dx), f) for dx in (1, 2, 3)]
    greet([sib, zdev, up, down, fdev] + xs)
    count = [0]

    def remote(src, dst, device):
        i = count[0]
        count[0] += 1
        copy = pltpu.make_async_remote_copy(
            src_ref=src, dst_ref=dst, send_sem=send.at[i], recv_sem=recv.at[i], device_id=device, device_id_type=MESH
        )
        copy.start()
        return copy

    nears = []

    def local(src, dst):
        copy = pltpu.make_async_copy(src, dst, near.at[len(nears)])
        copy.start()
        nears.append(copy)
        return copy

    own = rows_of(k, 128)
    mine4, theirs4 = rows_of(k, 4096), rows_of(1 - k, 4096)
    mine, theirs = rows_of(k, 512), rows_of(1 - k, 512)
    at = pl.ds(pl.multiple_of(1024 + k * 128, 128), 128)
    kv = [
        remote(k_ref.at[:, theirs], slab_ref.at[0, at, :], sib),
        remote(v_ref.at[:, theirs], slab_ref.at[1, at, :], sib),
    ]
    kv_near = [local(k_ref.at[:, mine], slab_ref.at[0, at, :]), local(v_ref.at[:, mine], slab_ref.at[1, at, :])]
    quarter = pl.ds(pl.multiple_of(k * 1024 + x * 256, 256), 256)
    w0 = remote(w_ref.at[quarter, :], wx_ref.at[rows_of(x), :], fdev)
    ins = []
    for dx in (1, 2, 3):
        cols = rows_of(lax.rem(x + dx, 4), 1024)
        ins.append(remote(in_ref.at[:, cols], inx_ref.at[x, own, :], xs[dx - 1]))
    qs = [
        remote(q_ref.at[:, theirs4], qx_ref.at[own, :], sib),
        remote(do_ref.at[:, theirs4], dox_ref.at[own, :], sib),
        remote(in_ref.at[:, rows_of(x, 1024)], inx_ref.at[x, own, :], sib),
    ]
    local(q_ref.at[:, mine4], qx_ref.at[own, :])
    local(do_ref.at[:, mine4], dox_ref.at[own, :])
    local(in_ref.at[:, rows_of(x, 1024)], inx_ref.at[x, own, :])

    def block(index):
        return slab_ref.at[:, rows_of(index), :]

    for c in kv:
        c.wait_recv()
    for c in kv_near:
        c.wait()
    y0 = remote(block(4), block(2), up)
    y0.wait_recv()
    y1 = remote(block(2), block(0), up)
    z0 = remote(block(4 - 2 * zl), block(3), zdev)
    w0.wait_recv()
    ws = [remote(wx_ref.at[rows_of(x), :], wx_ref.at[rows_of(x), :], xs[dx - 1]) for dx in (1, 2, 3)]
    y1.wait_recv()
    z1 = remote(block(2 - 2 * zl), block(1), zdev)
    shared = []
    for dx in (1, 2, 3):
        ins[dx - 1].wait_recv()
        piece = inx_ref.at[lax.rem(x + 4 - dx, 4), own, :]
        shared.append(remote(piece, piece, sib))
    for c in nears[2:]:
        c.wait()
    for c in qs + ws + shared + [z0, z1]:
        c.wait_recv()
    for c in kv + [w0] + ins + qs + [y0, y1, z0, z1] + ws + shared:
        c.wait_send()


def gather(queries, out_grad, keys, values, inputs, weight):
    messages = 20
    return pl.pallas_call(
        gather_kernel,
        out_shape=[
            jax.ShapeDtypeStruct((T, 4096), bf16),
            jax.ShapeDtypeStruct((T, 4096), bf16),
            jax.ShapeDtypeStruct((2, W, 512), bf16),
            jax.ShapeDtypeStruct((4, T, 1024), bf16),
            jax.ShapeDtypeStruct((1024, 1024), bf16),
        ],
        in_specs=[ANY] * 6,
        out_specs=[ANY] * 5,
        scratch_shapes=[
            pltpu.SemaphoreType.DMA((messages,)),
            pltpu.SemaphoreType.DMA((messages,)),
            pltpu.SemaphoreType.DMA((5,)),
        ],
        compiler_params=pltpu.CompilerParams(collective_id=0, has_side_effects=True),
        name="gather",
    )(queries, out_grad, keys, values, inputs, weight)


def attend(q, do, k_ref, v_ref, kt_ref, bias_ref, s_ref, dp_ref, p_ref, ds_ref):
    s_ref[...] = lax.dot_general(k_ref[...], q, NT, preferred_element_type=f32)
    dp_ref[...] = lax.dot_general(v_ref[...], do, NT, preferred_element_type=f32)
    step = 128
    top = None
    for i in range(0, W, step):
        s = s_ref[i : i + step, :] + bias_ref[i : i + step, :]
        t = jnp.max(s.reshape(step // 8, 8, T), axis=0)
        top = t if top is None else jnp.maximum(top, t)
    top = jnp.max(top, axis=0, keepdims=True)
    total = delta = 0.0
    for i in range(0, W, step):
        e = jnp.exp2((s_ref[i : i + step, :] + bias_ref[i : i + step, :] - top) * EXP2)
        p_ref[i : i + step, :] = e.astype(bf16)
        total += jnp.sum(e.reshape(step // 8, 8, T), axis=0)
        delta += jnp.sum((e * dp_ref[i : i + step, :]).reshape(step // 8, 8, T), axis=0)
    inverse = 1.0 / jnp.sum(total, axis=0, keepdims=True)
    delta = jnp.sum(delta, axis=0, keepdims=True) * inverse
    for i in range(0, W, step):
        e = p_ref[i : i + step, :].astype(f32)
        ds_ref[i : i + step, :] = (e * (dp_ref[i : i + step, :] - delta)).astype(bf16)
    dq = jnp.dot(kt_ref[...], ds_ref[...], preferred_element_type=f32) * (inverse * SCALE)
    return dq.T, jnp.broadcast_to(inverse, (D, T)).T


def attention_kernel(
    key_doc, query_doc, q_ref, do_ref, k_ref, v_ref, dq_ref, dkv_ref, kt_ref, bias_ref, *scratch
):
    g, j = pl.program_id(0), pl.program_id(1)

    @pl.when((g == 0) & (j == 0))
    def _():
        key_at = lax.broadcasted_iota(jnp.int32, (W, T), 0)
        query_at = lax.broadcasted_iota(jnp.int32, (W, T), 1)
        allowed = (key_doc[...] == query_doc[...]) & (key_at <= query_at + (W - T))
        bias_ref[...] = jnp.where(allowed, 0.0, -1e30).astype(f32)

    @pl.when(j == 0)
    def _():
        kt_ref[...] = k_ref[...].T
        dkv_ref[...] = jnp.zeros_like(dkv_ref)

    for a in range(HB):
        cols = slice(a * D, (a + 1) * D)
        q, do = q_ref[:, cols], do_ref[:, cols]
        s_ref, dp_ref, p_ref, ds_ref = scratch[4 * a : 4 * a + 4]
        dq, inverse = attend(q, do, k_ref, v_ref, kt_ref, bias_ref, s_ref, dp_ref, p_ref, ds_ref)
        dq_ref[:, cols] = dq.astype(bf16)
        dkv_ref[0, 0] += jnp.dot(ds_ref[...], (q * inverse).astype(bf16), preferred_element_type=f32)
        dkv_ref[0, 1] += jnp.dot(p_ref[...], (do * inverse).astype(bf16), preferred_element_type=f32)


def attention(key_doc, query_doc, q, do, slab):
    n = 8 // HB
    scratch = []
    for _ in range(HB):
        scratch += [pltpu.VMEM((W, T), t) for t in (f32, f32, bf16, bf16)]
    heads = pl.BlockSpec((T, HB * D), lambda g, j: (0, g * n + j))
    return pl.pallas_call(
        attention_kernel,
        grid=(HALF, n),
        in_specs=[
            pl.BlockSpec((W, 1), lambda g, j: (0, 0)),
            pl.BlockSpec((1, T), lambda g, j: (0, 0)),
            heads,
            heads,
            pl.BlockSpec((None, W, D), lambda g, j: (0, 0, g)),
            pl.BlockSpec((None, W, D), lambda g, j: (1, 0, g)),
        ],
        out_specs=[heads, pl.BlockSpec((1, 2, W, D), lambda g, j: (g, 0, 0, 0))],
        out_shape=[jax.ShapeDtypeStruct((T, 4096), bf16), jax.ShapeDtypeStruct((HALF, 2, W, D), f32)],
        scratch_shapes=[pltpu.VMEM((D, W), bf16), pltpu.VMEM((W, T), f32)] + scratch,
        compiler_params=pltpu.CompilerParams(vmem_limit_bytes=50 * 2**20),
        name="attention",
    )(key_doc, query_doc, q, do, slab, slab)


def reduce_kernel(
    dkv_ref, dq_ref, inx_ref, w_ref, wx_ref,
    gq_ref, gk_ref, gv_ref, gi_ref, gw_ref,
    zsend, zrecv, ysend, yrecv, gkcat, gvcat, gx, wk, gibuf, gw_send, gw_recv, gw_own, zst, rz, last, fin, last_recv,
    send, recv, near,
):
    p, f, x, y, zl, k = position()
    sib = (p + 1 - 2 * k, f)
    zp = p + 2 - 4 * zl
    zdev = (zp, f)
    up, down = (wrapped(p, 4), f), (wrapped(p, -4), f)
    xs = [(along_x(p, dx), f) for dx in (1, 2, 3)]
    ys = [(along_y(p, y, dy), f) for dy in (1, 2, 3)]
    zs = [(p, 1 - f), (zp, f), (zp, 1 - f)]
    greet([sib, up, down] + xs + ys + zs)
    sent = []

    def remote(src, dst, device):
        i = len(sent)
        copy = pltpu.make_async_remote_copy(
            src_ref=src, dst_ref=dst, send_sem=send.at[i], recv_sem=recv.at[i], device_id=device, device_id_type=MESH
        )
        copy.start()
        sent.append(copy)
        return copy

    mine4 = rows_of(k, 4096)
    own, other = rows_of(k, 128), rows_of(1 - k, 128)
    near_gq = pltpu.make_async_copy(dq_ref.at[own, :], gq_ref.at[:, mine4], near.at[0])
    near_gq.start()
    near_w = pltpu.make_async_copy(w_ref.at[rows_of(k, 1024), :], wk, near.at[1])
    near_w.start()
    last_waits = [remote(dq_ref.at[other, :], gq_ref.at[:, mine4], sib)]

    def block(index):
        return slice(index * T, (index + 1) * T)

    first = []
    for g in range(HALF):
        for a, index in enumerate((3, 1)):
            zsend[g, a] = dkv_ref[g, :, block(index), :].astype(bf16)
        first.append(remote(zsend.at[g], zrecv.at[g], zdev))
    upper = zl == 1
    second = []
    for g in range(HALF):
        first[g].wait_recv()
        r0, r1 = zrecv[g, 0].astype(f32), zrecv[g, 1].astype(f32)
        ysend[g, 0] = (dkv_ref[g, :, block(0), :] + jnp.where(upper, r1, 0.0)).astype(bf16)
        second.append(remote(ysend.at[g, 0], yrecv.at[g, 0], down))
    third = []
    for g in range(HALF):
        second[g].wait_recv()
        r0, r1 = zrecv[g, 0].astype(f32), zrecv[g, 1].astype(f32)
        part = dkv_ref[g, :, block(2), :] + jnp.where(upper, r0, r1) + yrecv[g, 0].astype(f32)
        ysend[g, 1] = part.astype(bf16)
        third.append(remote(ysend.at[g, 1], yrecv.at[g, 1], down))
    for g in range(HALF):
        third[g].wait_recv()
        r0 = zrecv[g, 0].astype(f32)
        part = dkv_ref[g, :, block(4), :] + jnp.where(upper, 0.0, r0) + yrecv[g, 1].astype(f32)
        cols = pl.ds(pl.multiple_of((HALF * k + g) * D, D), D)
        gkcat[:, cols] = (part[0] * SCALE).astype(bf16)
        grad = part[1].astype(bf16)
        gvcat[:, cols] = grad
        gx[g * D : (g + 1) * D, rows_of(x)] = part[1].T.astype(bf16)
    mine = rows_of(k, 512)
    across = [remote(c.at[:, mine], c.at[:, mine], sib) for c in (gvcat, gkcat)]
    gxs = [remote(gx.at[:, rows_of(x)], gx.at[:, rows_of(x)], xs[dx - 1]) for dx in (1, 2, 3)]
    for c in across:
        c.wait_recv()
    gk_ref[...] = gkcat[own, :]
    gv_ref[...] = gvcat[own, :]
    near_w.wait()
    outs = []
    for j, w in enumerate((wk, wx_ref)):
        cols = rows_of((f if j == 0 else 1 - f) * 2 + k, 1024)
        for i in range(0, 1024, 256):
            gibuf[j, :, i : i + 256] = lax.dot_general(
                gvcat[...], w[i : i + 256, :], NT, preferred_element_type=f32
            ).astype(bf16)
        here = pltpu.make_async_copy(gibuf.at[j, own, :], gi_ref.at[:, cols], near.at[2 + j])
        here.start()
        outs.append(here)
        last_waits.append(remote(gibuf.at[j, other, :], gi_ref.at[:, cols], sib))
    for c in gxs:
        c.wait_recv()
    gws = []
    for dy in (1, 2, 3, 0):
        cols = rows_of(lax.rem(y + dy, 4))
        part = jnp.dot(gx[...], inx_ref[:, cols], preferred_element_type=f32)
        if dy:
            gw_send[dy - 1] = part.astype(bf16)
            gws.append(remote(gw_send.at[dy - 1], gw_recv.at[dy - 1], ys[dy - 1]))
        else:
            gw_own[...] = part
    for c in gws:
        c.wait_recv()
    part = (gw_own[...] + gw_recv[0].astype(f32) + gw_recv[1].astype(f32) + gw_recv[2].astype(f32)).T
    part = part.reshape(2, 2, 2, 32, 512)
    for a in range(2):
        for c in range(2):
            zst[a, c] = part[a, :, c]
    rzs = []
    for j, device in enumerate(zs):
        to_z, to_f = (zl, 1 - zl, 1 - zl)[j], (1 - f, f, 1 - f)[j]
        last[j] = zst[to_z, to_f].astype(bf16)
        rzs.append(remote(last.at[j], rz.at[j], device))
    for c in rzs:
        c.wait_recv()
    done = zst[zl, f] + rz[0].astype(f32) + rz[1].astype(f32) + rz[2].astype(f32)
    fin[...] = done * (1.0 / math.sqrt(2 * 8192))
    final = remote(fin.at[1 - k], last_recv, sib)
    gw_ref[:, mine] = fin[k]
    final.wait_recv()
    gw_ref[:, rows_of(1 - k, 512)] = last_recv[...]
    near_gq.wait()
    for c in outs:
        c.wait()
    for c in last_waits:
        c.wait_recv()
    for c in sent:
        c.wait_send()


def reduce(dkv, dq, inx, weight, wx):
    messages = 27
    pair = (2, T, D)
    return pl.pallas_call(
        reduce_kernel,
        out_shape=[
            jax.ShapeDtypeStruct((128, 8192), bf16),
            jax.ShapeDtypeStruct((128, 1024), bf16),
            jax.ShapeDtypeStruct((128, 1024), bf16),
            jax.ShapeDtypeStruct((128, 4096), bf16),
            jax.ShapeDtypeStruct((32, 1024), f32),
        ],
        in_specs=[VMEM, ANY, VMEM, ANY, VMEM],
        out_specs=[ANY, VMEM, VMEM, ANY, VMEM],
        scratch_shapes=[
            pltpu.VMEM((HALF, 2) + pair, bf16),
            pltpu.VMEM((HALF, 2) + pair, bf16),
            pltpu.VMEM((HALF, 2) + pair, bf16),
            pltpu.VMEM((HALF, 2) + pair, bf16),
            pltpu.VMEM((T, 1024), bf16),
            pltpu.VMEM((T, 1024), bf16),
            pltpu.VMEM((512, 1024), bf16),
            pltpu.VMEM((1024, 1024), bf16),
            pltpu.VMEM((2, T, 1024), bf16),
            pltpu.VMEM((3, 512, T), bf16),
            pltpu.VMEM((3, 512, T), bf16),
            pltpu.VMEM((512, T), f32),
            pltpu.VMEM((2, 2, 2, 32, 512), f32),
            pltpu.VMEM((3, 2, 32, 512), bf16),
            pltpu.VMEM((3, 2, 32, 512), bf16),
            pltpu.VMEM((2, 32, 512), f32),
            pltpu.VMEM((32, 512), f32),
            pltpu.SemaphoreType.DMA((messages,)),
            pltpu.SemaphoreType.DMA((messages,)),
            pltpu.SemaphoreType.DMA((4,)),
        ],
        compiler_params=pltpu.CompilerParams(
            collective_id=1, has_side_effects=True, vmem_limit_bytes=50 * 2**20
        ),
        name="reduce",
    )(dkv, dq, inx, weight, wx)


def documents(lengths):
    chip = lax.axis_index("seq") // 2
    entry = jnp.arange(lengths.shape[0])
    bounds = jnp.sum(jnp.where(entry[None, :] <= entry[:, None], lengths[None, :], 0), axis=1)
    at = chip * T - (W - T) + jnp.arange(W, dtype=jnp.int32)
    ids = jnp.sum((at[:, None] >= bounds[None, :]).astype(jnp.int32), axis=1)
    return jnp.where(at < 0, -1, ids)


def local(queries, keys, values, out_grad, doc_lengths, inputs, value_weight):
    ids = documents(doc_lengths[0])
    qx, dox, slab, inx, wx = gather(queries[0], out_grad[0], keys[0], values[0], inputs[0], value_weight)
    dq, dkv = attention(ids[:, None], ids[None, W - T :], qx, dox, slab)
    gq, gk, gv, gi, gw = reduce(dkv, dq, inx.reshape(1024, 1024), value_weight, wx)
    return gq[None], gk[None], gv[None], gi[None], gw


def solution(mesh):
    tokens = P("fsdp", "seq", None)
    in_specs = (tokens, tokens, tokens, tokens, P("fsdp", None), tokens, P("fsdp", None))
    out_specs = (tokens, tokens, tokens, tokens, P(("seq", "fsdp"), None))
    return jax.shard_map(local, mesh=mesh, in_specs=in_specs, out_specs=out_specs, check_vma=False)
```

```python
import math

import jax
import jax.numpy as jnp
from jax import lax
from jax.experimental import pallas as pl
from jax.experimental.pallas import tpu as pltpu
from jax.sharding import PartitionSpec as P

D = 128
T = 256
W = 1280
HALF = 4
HB = 4
MESSAGES = 109
SCALE = 1.0 / math.sqrt(D)
EXP2 = math.log2(math.e) * SCALE
NT = (((1,), (1,)), ((), ()))
f32, bf16 = jnp.float32, jnp.bfloat16
MESH = pl.DeviceIdType.MESH
ANY = pl.BlockSpec(memory_space=pl.ANY)
VMEM = pl.BlockSpec(memory_space=pltpu.VMEM)


def position():
    p, f = lax.axis_index("seq"), lax.axis_index("fsdp")
    return p, f, p // 16, p // 4 % 4, p // 2 % 2, p % 2


def wrapped(p, by):
    return lax.rem(p + by + 64, 64)


def along_x(p, dx):
    return lax.rem(p + 16 * dx, 64)


def along_y(p, y, dy):
    return p - 4 * y + 4 * lax.rem(y + dy, 4)


def greet(devices):
    barrier = pltpu.get_barrier_semaphore()
    for device in devices:
        pl.semaphore_signal(barrier, inc=1, device_id=device, device_id_type=MESH)
    pl.semaphore_wait(barrier, len(devices))


def rows_of(index, size=T):
    return pl.ds(pl.multiple_of(index * size, size), size)


def attend(q, do, k_ref, v_ref, kt_ref, bias_ref, s_ref, dp_ref, p_ref, ds_ref):
    s_ref[...] = lax.dot_general(k_ref[...], q, NT, preferred_element_type=f32)
    dp_ref[...] = lax.dot_general(v_ref[...], do, NT, preferred_element_type=f32)
    step = 128
    top = None
    for i in range(0, W, step):
        s = s_ref[i : i + step, :] + bias_ref[i : i + step, :]
        t = jnp.max(s.reshape(step // 8, 8, T), axis=0)
        top = t if top is None else jnp.maximum(top, t)
    top = jnp.max(top, axis=0, keepdims=True)
    total = delta = 0.0
    for i in range(0, W, step):
        e = jnp.exp2((s_ref[i : i + step, :] + bias_ref[i : i + step, :] - top) * EXP2)
        p_ref[i : i + step, :] = e.astype(bf16)
        total += jnp.sum(e.reshape(step // 8, 8, T), axis=0)
        delta += jnp.sum((e * dp_ref[i : i + step, :]).reshape(step // 8, 8, T), axis=0)
    inverse = 1.0 / jnp.sum(total, axis=0, keepdims=True)
    delta = jnp.sum(delta, axis=0, keepdims=True) * inverse
    for i in range(0, W, step):
        e = p_ref[i : i + step, :].astype(f32)
        ds_ref[i : i + step, :] = (e * (dp_ref[i : i + step, :] - delta)).astype(bf16)
    dq = jnp.dot(kt_ref[...], ds_ref[...], preferred_element_type=f32) * (inverse * SCALE)
    return dq.T, jnp.broadcast_to(inverse, (D, T)).T


def kernel(
    key_doc, query_doc, q_in, do_in, k_in, v_in, in_ref, w_ref,
    gq_ref, gk_ref, gv_ref, gi_ref, gw_ref,
    qx, dox, slab, inx, wk, wx, dq, acc, kt, bias,
    zsend, zrecv, ysend, yrecv, cat, gx, gibuf, gw_send, gw_recv, gw_own, zst, last, rz, fin, last_recv,
    send, recv, near, *scratch,
):
    p, f, x, y, zl, k = position()
    sib = (p + 1 - 2 * k, f)
    zp = p + 2 - 4 * zl
    zdev = (zp, f)
    up, down = (wrapped(p, 4), f), (wrapped(p, -4), f)
    xs = [(along_x(p, dx), f) for dx in (1, 2, 3)]
    ys = [(along_y(p, y, dy), f) for dy in (1, 2, 3)]
    zs = [(p, 1 - f), (zp, f), (zp, 1 - f)]
    every, nears = [], []

    def remote(src, dst, device):
        i = len(every)
        copy = pltpu.make_async_remote_copy(
            src_ref=src, dst_ref=dst, send_sem=send.at[i], recv_sem=recv.at[i], device_id=device, device_id_type=MESH
        )
        every.append(copy)
        return copy

    def local(src, dst):
        copy = pltpu.make_async_copy(src, dst, near.at[len(nears)])
        nears.append(copy)
        return copy

    own, other = rows_of(k, 128), rows_of(1 - k, 128)
    here = pl.ds(pl.multiple_of(1024 + k * 128, 128), 128)

    def column(core, g, size):
        return rows_of(core * HALF + g, size)

    def window(g, index):
        return slab.at[g, :, rows_of(index), :]

    kv, kv_near, qs, q_near = [], [], [], []
    for g in range(HALF):
        kv.append([remote(a.at[:, column(1 - k, g, D)], slab.at[g, i, here, :], sib) for i, a in enumerate((k_in, v_in))])
        kv_near.append([local(a.at[:, column(k, g, D)], slab.at[g, i, here, :]) for i, a in enumerate((k_in, v_in))])
        cols = pl.ds(g * 1024, 1024)
        pairs = ((q_in, qx), (do_in, dox))
        qs.append([remote(a.at[:, column(1 - k, g, 1024)], b.at[own, cols], sib) for a, b in pairs])
        q_near.append([local(a.at[:, column(k, g, 1024)], b.at[own, cols]) for a, b in pairs])
    y0 = [remote(window(g, 4), window(g, 2), up) for g in range(HALF)]
    y1 = [remote(window(g, 2), window(g, 0), up) for g in range(HALF)]
    z0 = [remote(window(g, 4 - 2 * zl), window(g, 3), zdev) for g in range(HALF)]
    z1 = [remote(window(g, 2 - 2 * zl), window(g, 1), zdev) for g in range(HALF)]
    in_rows = pl.ds(pl.multiple_of(x * T + k * 128, 128), 128)
    ins, shared = [], []
    for dx in (1, 2, 3):
        ins.append(remote(in_ref.at[:, rows_of(lax.rem(x + dx, 4), 1024)], inx.at[in_rows, :], xs[dx - 1]))
    for dx in (1, 2, 3):
        piece = inx.at[pl.ds(pl.multiple_of(lax.rem(x + 4 - dx, 4) * T + k * 128, 128), 128), :]
        shared.append(remote(piece, piece, sib))
    shared.append(remote(in_ref.at[:, rows_of(x, 1024)], inx.at[in_rows, :], sib))
    in_near = local(in_ref.at[:, rows_of(x, 1024)], inx.at[in_rows, :])
    w0 = remote(w_ref.at[pl.ds(pl.multiple_of(k * 1024 + x * T, T), T), :], wx.at[rows_of(x), :], (p, 1 - f))
    ws = [remote(wx.at[rows_of(x), :], wx.at[rows_of(x), :], device) for device in xs]
    w_near = local(w_ref.at[rows_of(k, 1024), :], wk)
    steps = 8 // HB * HALF
    width = HB * D
    gqs = [
        remote(dq.at[other, pl.ds(n * width, width)], gq_ref.at[:, pl.ds(pl.multiple_of(k * 4096 + n * width, width), width)], sib)
        for n in range(steps)
    ]
    gq_near = [
        local(dq.at[own, pl.ds(n * width, width)], gq_ref.at[:, pl.ds(pl.multiple_of(k * 4096 + n * width, width), width)])
        for n in range(steps)
    ]
    zc = [remote(zsend.at[g], zrecv.at[g], zdev) for g in range(HALF)]
    yc = [[remote(ysend.at[g, i], yrecv.at[g, i], down) for i in range(2)] for g in range(HALF)]
    across = [remote(cat.at[:, :, column(k, g, D)], cat.at[:, :, column(k, g, D)], sib) for g in range(HALF)]
    gxs = [[remote(gx.at[g, :, rows_of(x)], gx.at[g, :, rows_of(x)], device) for device in xs] for g in range(HALF)]
    gws = [[remote(gw_send.at[g, i], gw_recv.at[g, i], device) for i, device in enumerate(ys)] for g in range(HALF)]
    rzs = [[remote(last.at[g, i], rz.at[g, i], device) for i, device in enumerate(zs)] for g in range(HALF)]
    fins = [remote(fin.at[g, 1 - k], last_recv.at[g], sib) for g in range(HALF)]
    gi_cols = [rows_of((f if j == 0 else 1 - f) * 2 + k, 1024) for j in range(2)]
    gis = [remote(gibuf.at[j, other, :], gi_ref.at[:, gi_cols[j]], sib) for j in range(2)]
    gi_near = [local(gibuf.at[j, own, :], gi_ref.at[:, gi_cols[j]]) for j in range(2)]

    def start(copies):
        for c in copies:
            c.start()

    def arrived(copies):
        for c in copies:
            c.wait_recv()

    def ended(copies):
        for c in copies:
            c.wait()

    greet([sib, up, down] + xs + ys + zs)
    for g in range(HALF):
        start(kv[g] + kv_near[g])
        if g == 0:
            start(qs[0] + q_near[0])
    for g in range(1, HALF):
        start(qs[g] + q_near[g])
    start([w0, w_near, in_near, shared[3]] + ins)

    key_at = lax.broadcasted_iota(jnp.int32, (W, T), 0)
    query_at = lax.broadcasted_iota(jnp.int32, (W, T), 1)
    allowed = (key_doc[...] == query_doc[...]) & (key_at <= query_at + (W - T))
    bias[...] = jnp.where(allowed, 0.0, -1e30).astype(f32)

    def own_keys(g):
        arrived(kv[g])
        ended(kv_near[g])
        start([y0[g]])

    def pass_on(g):
        arrived([y0[g]])
        start([y1[g], z0[g]])

    def pass_last(g):
        arrived([y1[g]])
        start([z1[g]])

    def ready(g):
        arrived([z0[g], z1[g]] + qs[g])
        ended(q_near[g])

    own_keys(0)
    own_keys(1)
    pass_on(0)
    pass_on(1)
    pass_last(0)
    own_keys(2)
    own_keys(3)
    ready(0)

    def share_inputs():
        arrived(ins)
        start(shared[:3])

    def inputs_ready():
        arrived(shared)
        ended([in_near])

    def share_weight():
        arrived([w0])
        start(ws)

    before = {
        1: [lambda: pass_last(1), lambda: pass_on(2), lambda: pass_on(3)],
        2: [lambda: ready(1), lambda: pass_last(2), lambda: pass_last(3), share_weight],
        3: [share_inputs],
        4: [lambda: ready(2), inputs_ready],
        6: [lambda: ready(3)],
    }

    def block(index):
        return slice(index * T, (index + 1) * T)

    upper = zl == 1

    def back_z(g):
        for a, index in enumerate((3, 1)):
            zsend[g, a] = acc[g, :, block(index), :].astype(bf16)
        start([zc[g]])

    def back_y(g):
        arrived([zc[g]])
        ysend[g, 0] = (acc[g, :, block(0), :] + jnp.where(upper, zrecv[g, 1].astype(f32), 0.0)).astype(bf16)
        start([yc[g][0]])

    def back_yy(g):
        r0, r1 = zrecv[g, 0].astype(f32), zrecv[g, 1].astype(f32)
        arrived([yc[g][0]])
        part = acc[g, :, block(2), :] + jnp.where(upper, r0, r1) + yrecv[g, 0].astype(f32)
        ysend[g, 1] = part.astype(bf16)
        start([yc[g][1]])

    def owned(g):
        arrived([yc[g][1]])
        part = acc[g, :, block(4), :] + jnp.where(upper, 0.0, zrecv[g, 0].astype(f32)) + yrecv[g, 1].astype(f32)
        cat[0, :, column(k, g, D)] = (part[0] * SCALE).astype(bf16)
        cat[1, :, column(k, g, D)] = part[1].astype(bf16)
        gx[g, :, rows_of(x)] = part[1].T.astype(bf16)
        start(gxs[g] + [across[g]])

    def weight_part(g):
        arrived(gxs[g])
        for dy in (1, 2, 3, 0):
            part = jnp.dot(gx[g], inx[:, rows_of(lax.rem(y + dy, 4))], preferred_element_type=f32)
            if dy:
                gw_send[g, dy - 1] = part.astype(bf16)
                start([gws[g][dy - 1]])
            else:
                gw_own[g] = part

    def weight_y(g):
        arrived(gws[g])
        part = gw_own[g]
        for i in range(3):
            part += gw_recv[g, i].astype(f32)
        part = part.T.reshape(2, 2, 2, 32, D)
        for a in range(2):
            for c in range(2):
                zst[g, a, c] = part[a, :, c]
        for i in range(3):
            to_z, to_f = (zl, 1 - zl, 1 - zl)[i], (1 - f, f, 1 - f)[i]
            last[g, i] = zst[g, to_z, to_f].astype(bf16)
        start(rzs[g])

    def weight_z(g):
        arrived(rzs[g])
        part = zst[g, zl, f]
        for i in range(3):
            part += rz[g, i].astype(f32)
        fin[g] = part * (1.0 / math.sqrt(2 * 8192))
        start([fins[g]])

    stages = [back_z, back_y, back_yy, owned, weight_part, weight_y, weight_z]

    def after(n):
        per = steps // HALF
        return [(s, g) for s in range(len(stages)) for g in range(HALF) if n == per * (g + 1) - 1 + s]

    def body(step, carry):
        for n, acts in before.items():

            @pl.when(step == n)
            def _():
                for act in acts:
                    act()

        per = steps // HALF
        g, j = step // per, step % per

        @pl.when(j == 0)
        def _():
            kt[...] = slab[g, 0].T
            acc[g] = jnp.zeros((2, W, D), f32)

        for a in range(HB):
            cols = pl.ds(pl.multiple_of(step * width + a * D, D), D)
            q, do = qx[:, cols], dox[:, cols]
            s_ref, dp_ref, p_ref, ds_ref = scratch[4 * a : 4 * a + 4]
            grad, inverse = attend(q, do, slab.at[g, 0], slab.at[g, 1], kt, bias, s_ref, dp_ref, p_ref, ds_ref)
            dq[:, cols] = grad.astype(bf16)
            acc[g, 0] += jnp.dot(ds_ref[...], (q * inverse).astype(bf16), preferred_element_type=f32)
            acc[g, 1] += jnp.dot(p_ref[...], (do * inverse).astype(bf16), preferred_element_type=f32)

        for n in range(steps):

            @pl.when(step == n)
            def _():
                start([gqs[n], gq_near[n]])
                for s, g in after(n):
                    stages[s](g)

        return carry

    lax.fori_loop(0, steps, body, 0)

    def outputs():
        arrived(across + ws)
        ended([w_near])
        gk_ref[...] = cat[0, own, :]
        gv_ref[...] = cat[1, own, :]
        for j, w in enumerate((wk, wx)):
            for i in range(0, 1024, 256):
                gibuf[j, :, i : i + 256] = lax.dot_general(
                    cat[1], w[i : i + 256, :], NT, preferred_element_type=f32
                ).astype(bf16)
            start([gis[j], gi_near[j]])

    for n in range(steps, steps + len(stages) - 1):
        for s, g in after(n):
            if stages[s] is weight_part and g == HALF - 1:
                outputs()
            stages[s](g)
    for g in range(HALF):
        gw_ref[:, column(k, g, D)] = fin[g, k]
    arrived(fins)
    for g in range(HALF):
        gw_ref[:, column(1 - k, g, D)] = last_recv[g]
    arrived(gqs + gis)
    ended(gq_near + gi_near)
    for c in every:
        c.wait_send()


def backward(key_doc, query_doc, queries, out_grad, keys, values, inputs, weight):
    pair = (2, T, D)
    scratch = [
        pltpu.VMEM((T, 4096), bf16),
        pltpu.VMEM((T, 4096), bf16),
        pltpu.VMEM((HALF, 2, W, D), bf16),
        pltpu.VMEM((1024, 1024), bf16),
        pltpu.VMEM((1024, 1024), bf16),
        pltpu.VMEM((1024, 1024), bf16),
        pltpu.VMEM((T, 4096), bf16),
        pltpu.VMEM((HALF, 2, W, D), f32),
        pltpu.VMEM((D, W), bf16),
        pltpu.VMEM((W, T), f32),
        pltpu.VMEM((HALF, 2) + pair, bf16),
        pltpu.VMEM((HALF, 2) + pair, bf16),
        pltpu.VMEM((HALF, 2) + pair, bf16),
        pltpu.VMEM((HALF, 2) + pair, bf16),
        pltpu.VMEM((2, T, 1024), bf16),
        pltpu.VMEM((HALF, D, 1024), bf16),
        pltpu.VMEM((2, T, 1024), bf16),
        pltpu.VMEM((HALF, 3, D, T), bf16),
        pltpu.VMEM((HALF, 3, D, T), bf16),
        pltpu.VMEM((HALF, D, T), f32),
        pltpu.VMEM((HALF, 2, 2, 2, 32, D), f32),
        pltpu.VMEM((HALF, 3, 2, 32, D), bf16),
        pltpu.VMEM((HALF, 3, 2, 32, D), bf16),
        pltpu.VMEM((HALF, 2, 32, D), f32),
        pltpu.VMEM((HALF, 32, D), f32),
        pltpu.SemaphoreType.DMA((MESSAGES,)),
        pltpu.SemaphoreType.DMA((MESSAGES,)),
        pltpu.SemaphoreType.DMA((28,)),
    ]
    for _ in range(HB):
        scratch += [pltpu.VMEM((W, T), t) for t in (f32, f32, bf16, bf16)]
    return pl.pallas_call(
        kernel,
        out_shape=[
            jax.ShapeDtypeStruct((128, 8192), bf16),
            jax.ShapeDtypeStruct((128, 1024), bf16),
            jax.ShapeDtypeStruct((128, 1024), bf16),
            jax.ShapeDtypeStruct((128, 4096), bf16),
            jax.ShapeDtypeStruct((32, 1024), f32),
        ],
        in_specs=[VMEM, VMEM] + [ANY] * 6,
        out_specs=[ANY, VMEM, VMEM, ANY, VMEM],
        scratch_shapes=scratch,
        compiler_params=pltpu.CompilerParams(collective_id=0, has_side_effects=True, vmem_limit_bytes=60 * 2**20),
        name="backward",
    )(key_doc, query_doc, queries, out_grad, keys, values, inputs, weight)


def documents(lengths):
    chip = lax.axis_index("seq") // 2
    entry = jnp.arange(lengths.shape[0])
    bounds = jnp.sum(jnp.where(entry[None, :] <= entry[:, None], lengths[None, :], 0), axis=1)
    at = chip * T - (W - T) + jnp.arange(W, dtype=jnp.int32)
    ids = jnp.sum((at[:, None] >= bounds[None, :]).astype(jnp.int32), axis=1)
    return jnp.where(at < 0, -1, ids)


def local(queries, keys, values, out_grad, doc_lengths, inputs, value_weight):
    ids = documents(doc_lengths[0])
    gq, gk, gv, gi, gw = backward(
        ids[:, None], ids[None, W - T :], queries[0], out_grad[0], keys[0], values[0], inputs[0], value_weight
    )
    return gq[None], gk[None], gv[None], gi[None], gw


def solution(mesh):
    tokens = P("fsdp", "seq", None)
    in_specs = (tokens, tokens, tokens, tokens, P("fsdp", None), tokens, P("fsdp", None))
    out_specs = (tokens, tokens, tokens, tokens, P(("seq", "fsdp"), None))
    return jax.shard_map(local, mesh=mesh, in_specs=in_specs, out_specs=out_specs, check_vma=False)
```

```python
import math

import jax
import jax.numpy as jnp
from jax import lax
from jax.experimental import pallas as pl
from jax.experimental.pallas import tpu as pltpu
from jax.sharding import PartitionSpec as P

D = 128
T = 256
W = 1280
HALF = 4
HB = 4
MESSAGES = 114
SCALE = 1.0 / math.sqrt(D)
EXP2 = math.log2(math.e) * SCALE
NT = (((1,), (1,)), ((), ()))
f32, bf16 = jnp.float32, jnp.bfloat16
MESH = pl.DeviceIdType.MESH
ANY = pl.BlockSpec(memory_space=pl.ANY)
VMEM = pl.BlockSpec(memory_space=pltpu.VMEM)


def position():
    p, f = lax.axis_index("seq"), lax.axis_index("fsdp")
    return p, f, p // 16, p // 4 % 4, p // 2 % 2, p % 2


def wrapped(p, by):
    return lax.rem(p + by + 64, 64)


def along_x(p, dx):
    return lax.rem(p + 16 * dx, 64)


def along_y(p, y, dy):
    return p - 4 * y + 4 * lax.rem(y + dy, 4)


def greet(devices):
    barrier = pltpu.get_barrier_semaphore()
    for device in devices:
        pl.semaphore_signal(barrier, inc=1, device_id=device, device_id_type=MESH)
    pl.semaphore_wait(barrier, len(devices))


def rows_of(index, size=T):
    return pl.ds(pl.multiple_of(index * size, size), size)


def attend(q, do, k_ref, v_ref, kt_ref, bias_ref, s_ref, dp_ref, p_ref, ds_ref):
    s_ref[...] = lax.dot_general(k_ref[...], q, NT, preferred_element_type=f32)
    dp_ref[...] = lax.dot_general(v_ref[...], do, NT, preferred_element_type=f32)
    step = 128
    top = None
    for i in range(0, W, step):
        s = s_ref[i : i + step, :] + bias_ref[i : i + step, :]
        t = jnp.max(s.reshape(step // 8, 8, T), axis=0)
        top = t if top is None else jnp.maximum(top, t)
    top = jnp.max(top, axis=0, keepdims=True)
    total = delta = 0.0
    for i in range(0, W, step):
        e = jnp.exp2((s_ref[i : i + step, :] + bias_ref[i : i + step, :] - top) * EXP2)
        p_ref[i : i + step, :] = e.astype(bf16)
        total += jnp.sum(e.reshape(step // 8, 8, T), axis=0)
        delta += jnp.sum((e * dp_ref[i : i + step, :]).reshape(step // 8, 8, T), axis=0)
    inverse = 1.0 / jnp.sum(total, axis=0, keepdims=True)
    delta = jnp.sum(delta, axis=0, keepdims=True) * inverse
    for i in range(0, W, step):
        e = p_ref[i : i + step, :].astype(f32)
        ds_ref[i : i + step, :] = (e * (dp_ref[i : i + step, :] - delta)).astype(bf16)
    dq = jnp.dot(kt_ref[...], ds_ref[...], preferred_element_type=f32) * (inverse * SCALE)
    return dq.T, jnp.broadcast_to(inverse, (D, T)).T


def kernel(
    key_doc, query_doc, q_in, do_in, k_in, v_in, in_ref, w_ref,
    gq_ref, gk_ref, gv_ref, gi_ref, gw_ref,
    qx, dox, slab, inx, wk, dq, acc, kt, bias,
    zsend, zrecv, ysend, yrecv, cat, gx, gibuf, gw_send, gw_recv, gw_own, zst, last, rz, fin, last_recv,
    send, recv, near, *scratch,
):
    p, f, x, y, zl, k = position()
    sib = (p + 1 - 2 * k, f)
    zp = p + 2 - 4 * zl
    zdev = (zp, f)
    up, down = (wrapped(p, 4), f), (wrapped(p, -4), f)
    xs = [(along_x(p, dx), f) for dx in (1, 2, 3)]
    ys = [(along_y(p, y, dy), f) for dy in (1, 2, 3)]
    zs = [(p, 1 - f), (zp, f), (zp, 1 - f)]
    every, nears = [], []

    def remote(src, dst, device):
        i = len(every)
        copy = pltpu.make_async_remote_copy(
            src_ref=src, dst_ref=dst, send_sem=send.at[i], recv_sem=recv.at[i], device_id=device, device_id_type=MESH
        )
        every.append(copy)
        return copy

    def local(src, dst):
        copy = pltpu.make_async_copy(src, dst, near.at[len(nears)])
        nears.append(copy)
        return copy

    own, other = rows_of(k, 128), rows_of(1 - k, 128)
    here = pl.ds(pl.multiple_of(1024 + k * 128, 128), 128)

    def column(core, g, size):
        return rows_of(core * HALF + g, size)

    def window(g, index):
        return slab.at[g, :, rows_of(index), :]

    kv, kv_near, qs, q_near = [], [], [], []
    for g in range(HALF):
        kv.append([remote(a.at[:, column(1 - k, g, D)], slab.at[g, i, here, :], sib) for i, a in enumerate((k_in, v_in))])
        kv_near.append([local(a.at[:, column(k, g, D)], slab.at[g, i, here, :]) for i, a in enumerate((k_in, v_in))])
        cols = pl.ds(g * 1024, 1024)
        pairs = ((q_in, qx), (do_in, dox))
        qs.append([remote(a.at[:, column(1 - k, g, 1024)], b.at[own, cols], sib) for a, b in pairs])
        q_near.append([local(a.at[:, column(k, g, 1024)], b.at[own, cols]) for a, b in pairs])
    y0 = [remote(window(g, 4), window(g, 2), up) for g in range(HALF)]
    y1 = [remote(window(g, 2), window(g, 0), up) for g in range(HALF)]
    z0 = [remote(window(g, 4 - 2 * zl), window(g, 3), zdev) for g in range(HALF)]
    z1 = [remote(window(g, 2 - 2 * zl), window(g, 1), zdev) for g in range(HALF)]
    in_rows = pl.ds(pl.multiple_of(x * T + k * 128, 128), 128)
    ins, shared = [], []
    for dx in (1, 2, 3):
        ins.append(remote(in_ref.at[:, rows_of(lax.rem(x + dx, 4), 1024)], inx.at[in_rows, :], xs[dx - 1]))
    for dx in (1, 2, 3):
        piece = inx.at[pl.ds(pl.multiple_of(lax.rem(x + 4 - dx, 4) * T + k * 128, 128), 128), :]
        shared.append(remote(piece, piece, sib))
    shared.append(remote(in_ref.at[:, rows_of(x, 1024)], inx.at[in_rows, :], sib))
    in_near = local(in_ref.at[:, rows_of(x, 1024)], inx.at[in_rows, :])
    w_near = local(w_ref.at[rows_of(k, 1024), :], wk)
    steps = 8 // HB * HALF
    width = HB * D
    gqs = [
        remote(dq.at[other, pl.ds(n * width, width)], gq_ref.at[:, pl.ds(pl.multiple_of(k * 4096 + n * width, width), width)], sib)
        for n in range(steps)
    ]
    gq_near = [
        local(dq.at[own, pl.ds(n * width, width)], gq_ref.at[:, pl.ds(pl.multiple_of(k * 4096 + n * width, width), width)])
        for n in range(steps)
    ]
    zc = [remote(zsend.at[g], zrecv.at[g], zdev) for g in range(HALF)]
    yc = [[remote(ysend.at[g, i], yrecv.at[g, i], down) for i in range(2)] for g in range(HALF)]
    first2 = pl.ds(0, 2)
    across = [remote(cat.at[first2, :, column(k, g, D)], cat.at[first2, :, column(k, g, D)], sib) for g in range(HALF)]
    cross = [remote(cat.at[1, :, column(k, g, D)], cat.at[2, :, column(k, g, D)], (p, 1 - f)) for g in range(HALF)]
    relay = [remote(cat.at[2, :, column(k, g, D)], cat.at[2, :, column(k, g, D)], sib) for g in range(HALF)]
    gxs = [[remote(gx.at[g, :, rows_of(x)], gx.at[g, :, rows_of(x)], device) for device in xs] for g in range(HALF)]
    gws = [[remote(gw_send.at[g, i], gw_recv.at[g, i], device) for i, device in enumerate(ys)] for g in range(HALF)]
    rzs = [[remote(last.at[g, i], rz.at[g, i], device) for i, device in enumerate(zs)] for g in range(HALF)]
    fins = [remote(fin.at[g, 1 - k], last_recv.at[g], sib) for g in range(HALF)]
    gi_cols = rows_of(f * 2 + k, 1024)
    gis = [
        remote(gibuf.at[1, own, :], gi_ref.at[:, gi_cols], (p, 1 - f)),
        remote(gibuf.at[1, other, :], gi_ref.at[:, gi_cols], (p + 1 - 2 * k, 1 - f)),
        remote(gibuf.at[0, other, :], gi_ref.at[:, gi_cols], sib),
    ]
    gi_near = local(gibuf.at[0, own, :], gi_ref.at[:, gi_cols])

    def start(copies):
        for c in copies:
            c.start()

    def arrived(copies):
        for c in copies:
            c.wait_recv()

    def ended(copies):
        for c in copies:
            c.wait()

    greet([sib, up, down, (p + 1 - 2 * k, 1 - f)] + xs + ys + zs)
    for g in range(HALF):
        start(kv[g] + kv_near[g])
        if g == 0:
            start(qs[0] + q_near[0])
    for g in range(1, HALF):
        start(qs[g] + q_near[g])
    start([w_near, in_near])

    key_at = lax.broadcasted_iota(jnp.int32, (W, T), 0)
    query_at = lax.broadcasted_iota(jnp.int32, (W, T), 1)
    allowed = (key_doc[...] == query_doc[...]) & (key_at <= query_at + (W - T))
    bias[...] = jnp.where(allowed, 0.0, -1e30).astype(f32)

    def own_keys(g):
        arrived(kv[g])
        ended(kv_near[g])
        start([y0[g]])

    def pass_on(g):
        arrived([y0[g]])
        start([y1[g], z0[g]])

    def pass_last(g):
        arrived([y1[g]])
        start([z1[g]])

    def ready(g):
        arrived([z0[g], z1[g]] + qs[g])
        ended(q_near[g])

    own_keys(0)
    own_keys(1)
    pass_on(0)
    pass_on(1)
    pass_last(0)
    own_keys(2)
    own_keys(3)
    ready(0)

    def share_inputs():
        arrived(ins)
        start(shared[:3])

    def inputs_ready():
        arrived(shared)
        ended([in_near])

    def send_inputs():
        start(ins + shared[3:])

    before = {
        1: [send_inputs, lambda: pass_last(1), lambda: pass_on(2), lambda: pass_on(3)],
        2: [lambda: ready(1), lambda: pass_last(2), lambda: pass_last(3)],
        3: [share_inputs],
        4: [lambda: ready(2), inputs_ready],
        6: [lambda: ready(3)],
    }

    def block(index):
        return slice(index * T, (index + 1) * T)

    upper = zl == 1

    def back_z(g):
        for a, index in enumerate((3, 1)):
            zsend[g, a] = acc[g, :, block(index), :].astype(bf16)
        start([zc[g]])

    def back_y(g):
        arrived([zc[g]])
        ysend[g, 0] = (acc[g, :, block(0), :] + jnp.where(upper, zrecv[g, 1].astype(f32), 0.0)).astype(bf16)
        start([yc[g][0]])

    def back_yy(g):
        r0, r1 = zrecv[g, 0].astype(f32), zrecv[g, 1].astype(f32)
        arrived([yc[g][0]])
        part = acc[g, :, block(2), :] + jnp.where(upper, r0, r1) + yrecv[g, 0].astype(f32)
        ysend[g, 1] = part.astype(bf16)
        start([yc[g][1]])

    def owned(g):
        arrived([yc[g][1]])
        part = acc[g, :, block(4), :] + jnp.where(upper, 0.0, zrecv[g, 0].astype(f32)) + yrecv[g, 1].astype(f32)
        cat[0, :, column(k, g, D)] = (part[0] * SCALE).astype(bf16)
        cat[1, :, column(k, g, D)] = part[1].astype(bf16)
        gx[g, :, rows_of(x)] = part[1].T.astype(bf16)
        start([across[g], cross[g]] + gxs[g])

    def weight_part(g):
        if g < HALF - 1:
            arrived([cross[g]])
            start([relay[g]])
        arrived(gxs[g])
        for dy in (1, 2, 3, 0):
            part = jnp.dot(gx[g], inx[:, rows_of(lax.rem(y + dy, 4))], preferred_element_type=f32)
            if dy:
                gw_send[g, dy - 1] = part.astype(bf16)
                start([gws[g][dy - 1]])
            else:
                gw_own[g] = part

    def weight_y(g):
        arrived(gws[g])
        part = gw_own[g]
        for i in range(3):
            part += gw_recv[g, i].astype(f32)
        part = part.T.reshape(2, 2, 2, 32, D)
        for a in range(2):
            for c in range(2):
                zst[g, a, c] = part[a, :, c]
        for i in range(3):
            to_z, to_f = (zl, 1 - zl, 1 - zl)[i], (1 - f, f, 1 - f)[i]
            last[g, i] = zst[g, to_z, to_f].astype(bf16)
        start(rzs[g])

    def weight_z(g):
        arrived(rzs[g])
        part = zst[g, zl, f]
        for i in range(3):
            part += rz[g, i].astype(f32)
        fin[g] = part * (1.0 / math.sqrt(2 * 8192))
        start([fins[g]])

    stages = [back_z, back_y, back_yy, owned, weight_part, weight_y, weight_z]

    def after(n):
        per = steps // HALF
        return [(s, g) for s in range(len(stages)) for g in range(HALF) if n == per * (g + 1) - 1 + s]

    def body(step, carry):
        for n, acts in before.items():

            @pl.when(step == n)
            def _():
                for act in acts:
                    act()

        per = steps // HALF
        g, j = step // per, step % per

        @pl.when(j == 0)
        def _():
            kt[...] = slab[g, 0].T
            acc[g] = jnp.zeros((2, W, D), f32)

        for a in range(HB):
            cols = pl.ds(pl.multiple_of(step * width + a * D, D), D)
            q, do = qx[:, cols], dox[:, cols]
            s_ref, dp_ref, p_ref, ds_ref = scratch[4 * a : 4 * a + 4]
            grad, inverse = attend(q, do, slab.at[g, 0], slab.at[g, 1], kt, bias, s_ref, dp_ref, p_ref, ds_ref)
            dq[:, cols] = grad.astype(bf16)
            acc[g, 0] += jnp.dot(ds_ref[...], (q * inverse).astype(bf16), preferred_element_type=f32)
            acc[g, 1] += jnp.dot(p_ref[...], (do * inverse).astype(bf16), preferred_element_type=f32)

        for n in range(steps):

            @pl.when(step == n)
            def _():
                start([gqs[n], gq_near[n]])
                for s, g in after(n):
                    stages[s](g)

        return carry

    lax.fori_loop(0, steps, body, 0)

    def outputs():
        arrived([cross[HALF - 1]])
        start([relay[HALF - 1]])
        ended([w_near])
        arrived(across + relay)
        for j in (1, 0):
            for i in range(0, 1024, 256):
                gibuf[j, :, i : i + 256] = lax.dot_general(
                    cat[1 + j], wk[i : i + 256, :], NT, preferred_element_type=f32
                ).astype(bf16)
            start(gis[:2] if j else [gis[2], gi_near])
        gk_ref[...] = cat[0, own, :]
        gv_ref[...] = cat[1, own, :]

    for n in range(steps, steps + len(stages) - 1):
        for s, g in after(n):
            if stages[s] is weight_part and g == HALF - 1:
                outputs()
            stages[s](g)
    for g in range(HALF):
        gw_ref[:, column(k, g, D)] = fin[g, k]
    arrived(fins)
    for g in range(HALF):
        gw_ref[:, column(1 - k, g, D)] = last_recv[g]
    arrived(gqs + gis)
    ended(gq_near + [gi_near])
    for c in every:
        c.wait_send()


def backward(key_doc, query_doc, queries, out_grad, keys, values, inputs, weight):
    pair = (2, T, D)
    scratch = [
        pltpu.VMEM((T, 4096), bf16),
        pltpu.VMEM((T, 4096), bf16),
        pltpu.VMEM((HALF, 2, W, D), bf16),
        pltpu.VMEM((1024, 1024), bf16),
        pltpu.VMEM((1024, 1024), bf16),
        pltpu.VMEM((T, 4096), bf16),
        pltpu.VMEM((HALF, 2, W, D), f32),
        pltpu.VMEM((D, W), bf16),
        pltpu.VMEM((W, T), f32),
        pltpu.VMEM((HALF, 2) + pair, bf16),
        pltpu.VMEM((HALF, 2) + pair, bf16),
        pltpu.VMEM((HALF, 2) + pair, bf16),
        pltpu.VMEM((HALF, 2) + pair, bf16),
        pltpu.VMEM((3, T, 1024), bf16),
        pltpu.VMEM((HALF, D, 1024), bf16),
        pltpu.VMEM((2, T, 1024), bf16),
        pltpu.VMEM((HALF, 3, D, T), bf16),
        pltpu.VMEM((HALF, 3, D, T), bf16),
        pltpu.VMEM((HALF, D, T), f32),
        pltpu.VMEM((HALF, 2, 2, 2, 32, D), f32),
        pltpu.VMEM((HALF, 3, 2, 32, D), bf16),
        pltpu.VMEM((HALF, 3, 2, 32, D), bf16),
        pltpu.VMEM((HALF, 2, 32, D), f32),
        pltpu.VMEM((HALF, 32, D), f32),
        pltpu.SemaphoreType.DMA((MESSAGES,)),
        pltpu.SemaphoreType.DMA((MESSAGES,)),
        pltpu.SemaphoreType.DMA((27,)),
    ]
    for _ in range(HB):
        scratch += [pltpu.VMEM((W, T), t) for t in (f32, f32, bf16, bf16)]
    return pl.pallas_call(
        kernel,
        out_shape=[
            jax.ShapeDtypeStruct((128, 8192), bf16),
            jax.ShapeDtypeStruct((128, 1024), bf16),
            jax.ShapeDtypeStruct((128, 1024), bf16),
            jax.ShapeDtypeStruct((128, 4096), bf16),
            jax.ShapeDtypeStruct((32, 1024), f32),
        ],
        in_specs=[VMEM, VMEM] + [ANY] * 6,
        out_specs=[ANY, VMEM, VMEM, ANY, VMEM],
        scratch_shapes=scratch,
        compiler_params=pltpu.CompilerParams(collective_id=0, has_side_effects=True, vmem_limit_bytes=60 * 2**20),
        name="backward",
    )(key_doc, query_doc, queries, out_grad, keys, values, inputs, weight)


def place_kernel(*refs):
    n = (len(refs) - 2) // 3
    inward = [pltpu.make_async_copy(refs[i], refs[2 * n + i], refs[-2].at[i]) for i in range(n)]
    outward = [pltpu.make_async_copy(refs[2 * n + i], refs[n + i], refs[-1].at[i]) for i in range(n)]
    for c in inward:
        c.start()
    for i, c in enumerate(inward):
        c.wait()
        outward[i].start()
    for c in outward:
        c.wait()


def place(arrays):
    n = len(arrays)
    return pl.pallas_call(
        place_kernel,
        out_shape=[jax.ShapeDtypeStruct(a.shape, a.dtype) for a in arrays],
        in_specs=[ANY] * n,
        out_specs=[ANY] * n,
        scratch_shapes=[pltpu.VMEM(a.shape, a.dtype) for a in arrays] + [pltpu.SemaphoreType.DMA((n,))] * 2,
        compiler_params=pltpu.CompilerParams(vmem_limit_bytes=16 * 2**20),
        name="place",
    )(*arrays)


def documents(lengths):
    chip = lax.axis_index("seq") // 2
    entry = jnp.arange(lengths.shape[0])
    bounds = jnp.sum(jnp.where(entry[None, :] <= entry[:, None], lengths[None, :], 0), axis=1)
    at = chip * T - (W - T) + jnp.arange(W, dtype=jnp.int32)
    ids = jnp.sum((at[:, None] >= bounds[None, :]).astype(jnp.int32), axis=1)
    return jnp.where(at < 0, -1, ids)


def local(queries, keys, values, out_grad, doc_lengths, inputs, value_weight):
    ids = documents(doc_lengths[0])
    arrays = backward(
        ids[:, None], ids[None, W - T :], queries[0], out_grad[0], keys[0], values[0], inputs[0], value_weight
    )
    gq, gk, gv, gi, gw = place(arrays)
    return gq[None], gk[None], gv[None], gi[None], gw


def solution(mesh):
    tokens = P("fsdp", "seq", None)
    in_specs = (tokens, tokens, tokens, tokens, P("fsdp", None), tokens, P("fsdp", None))
    out_specs = (tokens, tokens, tokens, tokens, P(("seq", "fsdp"), None))
    return jax.shard_map(local, mesh=mesh, in_specs=in_specs, out_specs=out_specs, check_vma=False)
```

```python
import math

import jax
import jax.numpy as jnp
from jax import lax
from jax.experimental import pallas as pl
from jax.experimental.pallas import tpu as pltpu
from jax.sharding import PartitionSpec as P

D = 128
T = 256
W = 1280
HALF = 4
HB = 4
MESSAGES = 130
SCALE = 1.0 / math.sqrt(D)
EXP2 = math.log2(math.e) * SCALE
NT = (((1,), (1,)), ((), ()))
f32, bf16 = jnp.float32, jnp.bfloat16
MESH = pl.DeviceIdType.MESH
ANY = pl.BlockSpec(memory_space=pl.ANY)
VMEM = pl.BlockSpec(memory_space=pltpu.VMEM)


def position():
    p, f = lax.axis_index("seq"), lax.axis_index("fsdp")
    return p, f, p // 16, p // 4 % 4, p // 2 % 2, p % 2


def wrapped(p, by):
    return lax.rem(p + by + 64, 64)


def along_x(p, dx):
    return lax.rem(p + 16 * dx, 64)


def along_y(p, y, dy):
    return p - 4 * y + 4 * lax.rem(y + dy, 4)


def greet(devices):
    barrier = pltpu.get_barrier_semaphore()
    for device in devices:
        pl.semaphore_signal(barrier, inc=1, device_id=device, device_id_type=MESH)
    pl.semaphore_wait(barrier, len(devices))


def rows_of(index, size=T):
    return pl.ds(pl.multiple_of(index * size, size), size)


def attend(q, do, k_ref, v_ref, kt_ref, bias_ref, s_ref, dp_ref, p_ref, ds_ref):
    s_ref[...] = lax.dot_general(k_ref[...], q, NT, preferred_element_type=f32)
    dp_ref[...] = lax.dot_general(v_ref[...], do, NT, preferred_element_type=f32)
    step = 128
    top = None
    for i in range(0, W, step):
        s = s_ref[i : i + step, :] + bias_ref[i : i + step, :]
        t = jnp.max(s.reshape(step // 8, 8, T), axis=0)
        top = t if top is None else jnp.maximum(top, t)
    top = jnp.max(top, axis=0, keepdims=True)
    total = delta = 0.0
    for i in range(0, W, step):
        e = jnp.exp2((s_ref[i : i + step, :] + bias_ref[i : i + step, :] - top) * EXP2)
        p_ref[i : i + step, :] = e.astype(bf16)
        total += jnp.sum(e.reshape(step // 8, 8, T), axis=0)
        delta += jnp.sum((e * dp_ref[i : i + step, :]).reshape(step // 8, 8, T), axis=0)
    inverse = 1.0 / jnp.sum(total, axis=0, keepdims=True)
    delta = jnp.sum(delta, axis=0, keepdims=True) * inverse
    for i in range(0, W, step):
        e = p_ref[i : i + step, :].astype(f32)
        ds_ref[i : i + step, :] = (e * (dp_ref[i : i + step, :] - delta)).astype(bf16)
    dq = jnp.dot(kt_ref[...], ds_ref[...], preferred_element_type=f32) * (inverse * SCALE)
    return dq.T, jnp.broadcast_to(inverse, (D, T)).T


def kernel(
    key_doc, query_doc, q_in, do_in, k_in, v_in, in_ref, w_ref,
    gq_ref, gk_ref, gv_ref, gi_ref, gw_ref,
    qx, dox, slab, inx, wk, dq, acc, kt, bias,
    zsend, zrecv, ysend, yrecv, cat, gx, gibuf, gw_send, gw_recv, gw_own, zst, last, rz, fin, last_recv,
    send, recv, near, *scratch,
):
    p, f, x, y, zl, k = position()
    sib = (p + 1 - 2 * k, f)
    zp = p + 2 - 4 * zl
    zdev = (zp, f)
    up, down = (wrapped(p, 4), f), (wrapped(p, -4), f)
    xs = [(along_x(p, dx), f) for dx in (1, 2, 3)]
    ys = [(along_y(p, y, dy), f) for dy in (1, 2, 3)]
    zs = [(p, 1 - f), (zp, f), (zp, 1 - f)]
    every, nears = [], []

    def remote(src, dst, device):
        i = len(every)
        copy = pltpu.make_async_remote_copy(
            src_ref=src, dst_ref=dst, send_sem=send.at[i], recv_sem=recv.at[i], device_id=device, device_id_type=MESH
        )
        every.append(copy)
        return copy

    def local(src, dst):
        copy = pltpu.make_async_copy(src, dst, near.at[len(nears)])
        nears.append(copy)
        return copy

    own, other = rows_of(k, 128), rows_of(1 - k, 128)
    here = pl.ds(pl.multiple_of(1024 + k * 128, 128), 128)

    def column(core, g, size):
        return rows_of(core * HALF + g, size)

    def window(g, index):
        return slab.at[g, :, rows_of(index), :]

    kv, kv_near, qs, q_near = [], [], [], []
    for g in range(HALF):
        kv.append([remote(a.at[:, column(1 - k, g, D)], slab.at[g, i, here, :], sib) for i, a in enumerate((k_in, v_in))])
        kv_near.append([local(a.at[:, column(k, g, D)], slab.at[g, i, here, :]) for i, a in enumerate((k_in, v_in))])
        cols = pl.ds(g * 1024, 1024)
        pairs = ((q_in, qx), (do_in, dox))
        qs.append([remote(a.at[:, column(1 - k, g, 1024)], b.at[own, cols], sib) for a, b in pairs])
        q_near.append([local(a.at[:, column(k, g, 1024)], b.at[own, cols]) for a, b in pairs])
    y0 = [remote(window(g, 4), window(g, 2), up) for g in range(HALF)]
    y1 = [remote(window(g, 2), window(g, 0), up) for g in range(HALF)]
    z0 = [remote(window(g, 4 - 2 * zl), window(g, 3), zdev) for g in range(HALF)]
    z1 = [remote(window(g, 2 - 2 * zl), window(g, 1), zdev) for g in range(HALF)]
    in_rows = pl.ds(pl.multiple_of(x * T + k * 128, 128), 128)
    ins, shared = [], []
    for dx in (1, 2, 3):
        ins.append(remote(in_ref.at[:, rows_of(lax.rem(x + dx, 4), 1024)], inx.at[in_rows, :], xs[dx - 1]))
    for dx in (1, 2, 3):
        piece = inx.at[pl.ds(pl.multiple_of(lax.rem(x + 4 - dx, 4) * T + k * 128, 128), 128), :]
        shared.append(remote(piece, piece, sib))
    shared.append(remote(in_ref.at[:, rows_of(x, 1024)], inx.at[in_rows, :], sib))
    in_near = local(in_ref.at[:, rows_of(x, 1024)], inx.at[in_rows, :])
    w_near = local(w_ref.at[rows_of(k, 1024), :], wk)
    steps = 8 // HB * HALF
    width = HB * D
    gqs = [
        remote(dq.at[other, pl.ds(n * width, width)], gq_ref.at[:, pl.ds(pl.multiple_of(k * 4096 + n * width, width), width)], sib)
        for n in range(steps)
    ]
    gq_near = [
        local(dq.at[own, pl.ds(n * width, width)], gq_ref.at[:, pl.ds(pl.multiple_of(k * 4096 + n * width, width), width)])
        for n in range(steps)
    ]
    zc = [[remote(zsend.at[g, c], zrecv.at[g, c], zdev) for c in range(2)] for g in range(HALF)]
    yc = [
        [[remote(ysend.at[g, i, c], yrecv.at[g, i, c], down) for c in range(2)] for i in range(2)] for g in range(HALF)
    ]
    across = [
        [remote(cat.at[c, :, column(k, g, D)], cat.at[c, :, column(k, g, D)], sib) for c in range(2)] for g in range(HALF)
    ]
    cross = [remote(cat.at[1, :, column(k, g, D)], cat.at[2, :, column(k, g, D)], (p, 1 - f)) for g in range(HALF)]
    relay = [remote(cat.at[2, :, column(k, g, D)], cat.at[2, :, column(k, g, D)], sib) for g in range(HALF)]
    gxs = [[remote(gx.at[g, :, rows_of(x)], gx.at[g, :, rows_of(x)], device) for device in xs] for g in range(HALF)]
    gws = [[remote(gw_send.at[g, i], gw_recv.at[g, i], device) for i, device in enumerate(ys)] for g in range(HALF)]
    rzs = [[remote(last.at[g, i], rz.at[g, i], device) for i, device in enumerate(zs)] for g in range(HALF)]
    fins = [remote(fin.at[g, 1 - k], last_recv.at[g], sib) for g in range(HALF)]
    gi_cols = rows_of(f * 2 + k, 1024)
    gis = [
        remote(gibuf.at[1, own, :], gi_ref.at[:, gi_cols], (p, 1 - f)),
        remote(gibuf.at[1, other, :], gi_ref.at[:, gi_cols], (p + 1 - 2 * k, 1 - f)),
        remote(gibuf.at[0, other, :], gi_ref.at[:, gi_cols], sib),
    ]
    gi_near = local(gibuf.at[0, own, :], gi_ref.at[:, gi_cols])

    def start(copies):
        for c in copies:
            c.start()

    def arrived(copies):
        for c in copies:
            c.wait_recv()

    def ended(copies):
        for c in copies:
            c.wait()

    greet([sib, up, down, (p + 1 - 2 * k, 1 - f)] + xs + ys + zs)
    for g in range(HALF):
        start(kv[g] + kv_near[g])
        if g == 0:
            start(qs[0] + q_near[0])
    for g in range(1, HALF):
        start(qs[g] + q_near[g])
    start([w_near, in_near])

    key_at = lax.broadcasted_iota(jnp.int32, (W, T), 0)
    query_at = lax.broadcasted_iota(jnp.int32, (W, T), 1)
    allowed = (key_doc[...] == query_doc[...]) & (key_at <= query_at + (W - T))
    bias[...] = jnp.where(allowed, 0.0, -1e30).astype(f32)

    def own_keys(g):
        arrived(kv[g])
        ended(kv_near[g])
        start([y0[g]])

    def pass_on(g):
        arrived([y0[g]])
        start([y1[g], z0[g]])

    def pass_last(g):
        arrived([y1[g]])
        start([z1[g]])

    def ready(g):
        arrived([z0[g], z1[g]] + qs[g])
        ended(q_near[g])

    own_keys(0)
    own_keys(1)
    pass_on(0)
    pass_on(1)
    pass_last(0)
    own_keys(2)
    own_keys(3)
    ready(0)

    def share_inputs():
        arrived(ins)
        start(shared[:3])

    def inputs_ready():
        arrived(shared)
        ended([in_near])

    def send_inputs():
        start(ins + shared[3:])

    before = {
        1: [send_inputs, lambda: pass_last(1), lambda: pass_on(2), lambda: pass_on(3)],
        2: [lambda: ready(1), lambda: pass_last(2), lambda: pass_last(3)],
        3: [share_inputs],
        4: [lambda: ready(2), inputs_ready],
        6: [lambda: ready(3)],
    }

    def block(index):
        return slice(index * T, (index + 1) * T)

    upper = zl == 1

    def back_z(g):
        for c in (1, 0):
            for a, index in enumerate((3, 1)):
                zsend[g, c, a] = acc[g, c, block(index), :].astype(bf16)
            start([zc[g][c]])

    def hop_y(g, c):
        arrived([zc[g][c]])
        ysend[g, 0, c] = (acc[g, c, block(0), :] + jnp.where(upper, zrecv[g, c, 1].astype(f32), 0.0)).astype(bf16)
        start([yc[g][0][c]])

    def hop_yy(g, c):
        arrived([yc[g][0][c]])
        r0, r1 = zrecv[g, c, 0].astype(f32), zrecv[g, c, 1].astype(f32)
        part = acc[g, c, block(2), :] + jnp.where(upper, r0, r1) + yrecv[g, 0, c].astype(f32)
        ysend[g, 1, c] = part.astype(bf16)
        start([yc[g][1][c]])

    def keep(g, c):
        arrived([yc[g][1][c]])
        r0 = jnp.where(upper, 0.0, zrecv[g, c, 0].astype(f32))
        part = acc[g, c, block(4), :] + r0 + yrecv[g, 1, c].astype(f32)
        if c:
            cat[1, :, column(k, g, D)] = part.astype(bf16)
            gx[g, :, rows_of(x)] = part.T.astype(bf16)
            start([across[g][1], cross[g]] + gxs[g])
        else:
            cat[0, :, column(k, g, D)] = (part * SCALE).astype(bf16)
            start([across[g][0]])

    def both(hop, g):
        for c in (1, 0) if g < HALF - 1 else (1,):
            hop(g, c)

    def back_y(g):
        both(hop_y, g)

    def back_yy(g):
        both(hop_yy, g)

    def owned(g):
        both(keep, g)
        if g == HALF - 1:
            hop_y(g, 0)

    def weight_part(g):
        if g < HALF - 1:
            arrived([cross[g]])
            start([relay[g]])
        arrived(gxs[g])
        for dy in (1, 2, 3, 0):
            part = jnp.dot(gx[g], inx[:, rows_of(lax.rem(y + dy, 4))], preferred_element_type=f32)
            if dy:
                gw_send[g, dy - 1] = part.astype(bf16)
                start([gws[g][dy - 1]])
            else:
                gw_own[g] = part

    def weight_y(g):
        arrived(gws[g])
        part = gw_own[g]
        for i in range(3):
            part += gw_recv[g, i].astype(f32)
        part = part.T.reshape(2, 2, 2, 32, D)
        for a in range(2):
            for c in range(2):
                zst[g, a, c] = part[a, :, c]
        for i in range(3):
            to_z, to_f = (zl, 1 - zl, 1 - zl)[i], (1 - f, f, 1 - f)[i]
            last[g, i] = zst[g, to_z, to_f].astype(bf16)
        start(rzs[g])

    def weight_z(g):
        arrived(rzs[g])
        part = zst[g, zl, f]
        for i in range(3):
            part += rz[g, i].astype(f32)
        fin[g] = part * (1.0 / math.sqrt(2 * 8192))
        start([fins[g]])

    stages = [back_z, back_y, back_yy, owned, weight_part, weight_y, weight_z]

    def after(n):
        per = steps // HALF
        return [(s, g) for s in range(len(stages)) for g in range(HALF) if n == per * (g + 1) - 1 + s]

    def body(step, carry):
        for n, acts in before.items():

            @pl.when(step == n)
            def _():
                for act in acts:
                    act()

        per = steps // HALF
        g, j = step // per, step % per

        @pl.when(j == 0)
        def _():
            kt[...] = slab[g, 0].T
            acc[g] = jnp.zeros((2, W, D), f32)

        for a in range(HB):
            cols = pl.ds(pl.multiple_of(step * width + a * D, D), D)
            q, do = qx[:, cols], dox[:, cols]
            s_ref, dp_ref, p_ref, ds_ref = scratch[4 * a : 4 * a + 4]
            grad, inverse = attend(q, do, slab.at[g, 0], slab.at[g, 1], kt, bias, s_ref, dp_ref, p_ref, ds_ref)
            dq[:, cols] = grad.astype(bf16)
            acc[g, 0] += jnp.dot(ds_ref[...], (q * inverse).astype(bf16), preferred_element_type=f32)
            acc[g, 1] += jnp.dot(p_ref[...], (do * inverse).astype(bf16), preferred_element_type=f32)

        for n in range(steps):

            @pl.when(step == n)
            def _():
                start([gqs[n], gq_near[n]])
                for s, g in after(n):
                    stages[s](g)

        return carry

    lax.fori_loop(0, steps, body, 0)

    def outputs():
        arrived([cross[HALF - 1]])
        start([relay[HALF - 1]])
        ended([w_near])
        arrived(relay + [c[1] for c in across])
        for j in (1, 0):
            for i in range(0, 1024, 256):
                gibuf[j, :, i : i + 256] = lax.dot_general(
                    cat[1 + j], wk[i : i + 256, :], NT, preferred_element_type=f32
                ).astype(bf16)
            start(gis[:2] if j else [gis[2], gi_near])
        gv_ref[...] = cat[1, own, :]

    for n in range(steps, steps + len(stages) - 1):
        for s, g in after(n):
            if stages[s] is weight_part and g == HALF - 1:
                outputs()
                hop_yy(g, 0)
            stages[s](g)
            if stages[s] is weight_part and g == HALF - 1:
                keep(g, 0)
    arrived([c[0] for c in across])
    gk_ref[...] = cat[0, own, :]
    for g in range(HALF):
        gw_ref[:, column(k, g, D)] = fin[g, k]
    arrived(fins)
    for g in range(HALF):
        gw_ref[:, column(1 - k, g, D)] = last_recv[g]
    arrived(gqs + gis)
    ended(gq_near + [gi_near])
    for c in every:
        c.wait_send()


def backward(key_doc, query_doc, queries, out_grad, keys, values, inputs, weight):
    pair = (2, T, D)
    scratch = [
        pltpu.VMEM((T, 4096), bf16),
        pltpu.VMEM((T, 4096), bf16),
        pltpu.VMEM((HALF, 2, W, D), bf16),
        pltpu.VMEM((1024, 1024), bf16),
        pltpu.VMEM((1024, 1024), bf16),
        pltpu.VMEM((T, 4096), bf16),
        pltpu.VMEM((HALF, 2, W, D), f32),
        pltpu.VMEM((D, W), bf16),
        pltpu.VMEM((W, T), f32),
        pltpu.VMEM((HALF, 2) + pair, bf16),
        pltpu.VMEM((HALF, 2) + pair, bf16),
        pltpu.VMEM((HALF, 2) + pair, bf16),
        pltpu.VMEM((HALF, 2) + pair, bf16),
        pltpu.VMEM((3, T, 1024), bf16),
        pltpu.VMEM((HALF, D, 1024), bf16),
        pltpu.VMEM((2, T, 1024), bf16),
        pltpu.VMEM((HALF, 3, D, T), bf16),
        pltpu.VMEM((HALF, 3, D, T), bf16),
        pltpu.VMEM((HALF, D, T), f32),
        pltpu.VMEM((HALF, 2, 2, 2, 32, D), f32),
        pltpu.VMEM((HALF, 3, 2, 32, D), bf16),
        pltpu.VMEM((HALF, 3, 2, 32, D), bf16),
        pltpu.VMEM((HALF, 2, 32, D), f32),
        pltpu.VMEM((HALF, 32, D), f32),
        pltpu.SemaphoreType.DMA((MESSAGES,)),
        pltpu.SemaphoreType.DMA((MESSAGES,)),
        pltpu.SemaphoreType.DMA((27,)),
    ]
    for _ in range(HB):
        scratch += [pltpu.VMEM((W, T), t) for t in (f32, f32, bf16, bf16)]
    return pl.pallas_call(
        kernel,
        out_shape=[
            jax.ShapeDtypeStruct((128, 8192), bf16),
            jax.ShapeDtypeStruct((128, 1024), bf16),
            jax.ShapeDtypeStruct((128, 1024), bf16),
            jax.ShapeDtypeStruct((128, 4096), bf16),
            jax.ShapeDtypeStruct((32, 1024), f32),
        ],
        in_specs=[VMEM, VMEM] + [ANY] * 6,
        out_specs=[ANY, VMEM, VMEM, ANY, VMEM],
        scratch_shapes=scratch,
        compiler_params=pltpu.CompilerParams(collective_id=0, has_side_effects=True, vmem_limit_bytes=60 * 2**20),
        name="backward",
    )(key_doc, query_doc, queries, out_grad, keys, values, inputs, weight)


def place_kernel(*refs):
    n = (len(refs) - 2) // 3
    inward = [pltpu.make_async_copy(refs[i], refs[2 * n + i], refs[-2].at[i]) for i in range(n)]
    outward = [pltpu.make_async_copy(refs[2 * n + i], refs[n + i], refs[-1].at[i]) for i in range(n)]
    for c in inward:
        c.start()
    for i, c in enumerate(inward):
        c.wait()
        outward[i].start()
    for c in outward:
        c.wait()


def place(arrays):
    n = len(arrays)
    return pl.pallas_call(
        place_kernel,
        out_shape=[jax.ShapeDtypeStruct(a.shape, a.dtype) for a in arrays],
        in_specs=[ANY] * n,
        out_specs=[ANY] * n,
        scratch_shapes=[pltpu.VMEM(a.shape, a.dtype) for a in arrays] + [pltpu.SemaphoreType.DMA((n,))] * 2,
        compiler_params=pltpu.CompilerParams(vmem_limit_bytes=16 * 2**20),
        name="place",
    )(*arrays)


def documents(lengths):
    chip = lax.axis_index("seq") // 2
    entry = jnp.arange(lengths.shape[0])
    bounds = jnp.sum(jnp.where(entry[None, :] <= entry[:, None], lengths[None, :], 0), axis=1)
    at = chip * T - (W - T) + jnp.arange(W, dtype=jnp.int32)
    ids = jnp.sum((at[:, None] >= bounds[None, :]).astype(jnp.int32), axis=1)
    return jnp.where(at < 0, -1, ids)


def local(queries, keys, values, out_grad, doc_lengths, inputs, value_weight):
    ids = documents(doc_lengths[0])
    arrays = backward(
        ids[:, None], ids[None, W - T :], queries[0], out_grad[0], keys[0], values[0], inputs[0], value_weight
    )
    gq, gk, gv, gi, gw = place(arrays)
    return gq[None], gk[None], gv[None], gi[None], gw


def solution(mesh):
    tokens = P("fsdp", "seq", None)
    in_specs = (tokens, tokens, tokens, tokens, P("fsdp", None), tokens, P("fsdp", None))
    out_specs = (tokens, tokens, tokens, tokens, P(("seq", "fsdp"), None))
    return jax.shard_map(local, mesh=mesh, in_specs=in_specs, out_specs=out_specs, check_vma=False)
```
